128 devices in a mesh: seq: 8 (over z, x_hi), dp: 16 (over y, x_lo, core).
Axes of the slice: x: 4 (x_hi: 2, x_lo: 2; x = x_hi * 2 + x_lo), y: 4, z: 4, core: 2. Of those that a mesh axis runs over, the one named last changes fastest.
Arguments:
- query_rows: bfloat16 [16, 6144, 1536], P('dp', 'seq'), may hold values from -8 to 8
- key_rows: bfloat16 [16, 6144, 1536], P('dp', 'seq'), may hold values from -8 to 8
- value_rows: bfloat16 [16, 6144, 1536], P('dp', 'seq'), may hold values from -6 to 6
- attention_out: bfloat16 [16, 6144, 1536], P('dp', 'seq'), may hold values from -6 to 6
- output_grad: bfloat16 [16, 6144, 3072], P('dp', 'seq'), may hold values from -6 to 6
- output_weight: bfloat16 [1536, 3072], P('dp'), may hold values from -0.15625 to 0.15625
- tile_mask: int32 [16, 16, 3], P('dp', 'seq'), may hold values from 0 to 1, as said below
- live_tiles: int32 [16, 8], P('dp'), may hold values from 1 to 2, as said below
Outputs:
- query_grad: bfloat16 [16, 6144, 1536], P('dp', 'seq')
- key_grad: bfloat16 [16, 6144, 1536], P('dp', 'seq')
- value_grad: bfloat16 [16, 6144, 1536], P('dp', 'seq')
- weight_grad: float32 [1536, 3072], P('dp')
The draws below stay inside these ranges and needn't reach their ends.
Inputs may be any that keep to these rules, and one draw needn't show every extreme that they name: `tile_mask`: 1 marks an attended neighbour; entry 1 (the tile itself) is always 1, and so is every entry that points into another slab; entries pointing outside the video are ignored. `live_tiles`: tiles of a slab at or beyond its count are padding; every sample has a slab with all 2 tiles live.
All inputs are finite; a program needn't handle non-finite values.
Results may differ from the reference program's by a relative error of at most 0.027.
Values may be sent and summed in bfloat16 or wider, within the bound.
No kernel may reach another device: no remote copies, remote signals or barrier semaphores. Data moves between devices by JAX's collectives and lax.ppermute only.
A program may use at most 320 MiB of HBM per device.

```python
import math
import jax
import jax.numpy as jnp
from jax import lax

D = 3072
HDIM = 128
TILE = 384
TT_DEV = 2
FEAT = 1536
TILES = 16
SEQ = 6144
SAMPLES = 16


def head_scales(row_key, low_scale, high_scale):
    heads = FEAT // HDIM
    drawn = jnp.exp(jax.random.uniform(row_key, (SAMPLES, SEQ, heads, 1), jnp.float32, math.log(low_scale), math.log(high_scale)))
    return jnp.broadcast_to(drawn, (SAMPLES, SEQ, heads, HDIM)).reshape(SAMPLES, SEQ, FEAT)


def draw_query_rows(key, part):
    key = jax.random.fold_in(key, 11)
    base_key, row_key = jax.random.split(key)
    base_field = jax.random.normal(base_key, (SAMPLES, SEQ, FEAT), jnp.float32)
    return jnp.clip(base_field * head_scales(row_key, 0.3, 3.0), -8.0, 8.0).astype(jnp.bfloat16)


def draw_key_rows(key, part):
    key = jax.random.fold_in(key, 13)
    base_key, row_key = jax.random.split(key)
    base_field = jax.random.normal(base_key, (SAMPLES, SEQ, FEAT), jnp.float32)
    return jnp.clip(base_field * head_scales(row_key, 0.8, 1.25), -8.0, 8.0).astype(jnp.bfloat16)


def draw_tile_mask(key, part):
    key = jax.random.fold_in(key, 23)
    random_bits = jax.random.randint(key, (SAMPLES, TILES, 3), 0, 2)
    local_tile = (jnp.arange(TILES, dtype=jnp.int32) % TT_DEV)[None, :, None]
    slot_index = jnp.arange(3, dtype=jnp.int32)[None, None, :]
    forced = (slot_index == 1) | (slot_index == 0) & (local_tile == 0) | (slot_index == 2) & (local_tile == TT_DEV - 1)
    return jnp.where(forced, 1, random_bits).astype(jnp.int32)


def draw_live_tiles(key, part):
    key = jax.random.fold_in(key, 37)
    full_key, short_key, pick_key = jax.random.split(key, 3)
    slabs = TILES // TT_DEV
    full_slab = jax.random.randint(full_key, (SAMPLES, slabs), 0, 4) > 0
    shorter = jax.random.randint(short_key, (SAMPLES, slabs), 1, TT_DEV + 1)
    pick_slab = jax.random.randint(pick_key, (SAMPLES, 1), 0, slabs)
    forced = jnp.arange(slabs, dtype=jnp.int32)[None, :] == pick_slab
    return jnp.where(full_slab | forced, TT_DEV, shorter).astype(jnp.int32)


def raised(entries, own_key, source, target, shards_of, factor):
    owner, partner = [(jnp.arange(entries.shape[dim]) // (entries.shape[dim] // shards_of)).reshape([-1 if axis == dim else 1 for axis in range(entries.ndim)]) for dim in (source, target)]
    chosen = jax.random.permutation(own_key, shards_of)[partner]
    strong = (owner == chosen) | (owner == (partner + shards_of // 2) % shards_of)
    return jnp.where(strong, factor * entries, entries)


def level_of(stream_key, shape, cuts, smallest, high):
    gain = 1.0
    for dim, parts in cuts:
        steps = jax.random.uniform(jax.random.fold_in(jax.random.fold_in(stream_key, 6), dim), (parts,), jnp.float32, smallest / len(cuts), high / len(cuts))
        gain = gain * jnp.repeat(jnp.exp(steps), shape[dim] // parts).reshape((-1,) + (1,) * (len(shape) - 1 - dim))
    return gain


def scatter_about(stream_key, shape, scale, bound, cuts=(), held_as=jnp.bfloat16):
    level = level_of(stream_key, shape, cuts, -0.22, 0.18) if cuts else 1.0
    entries = jax.random.normal(stream_key, shape, jnp.float32) * scale * level
    return jnp.minimum(jnp.maximum(entries, -bound), bound).astype(held_as)


def noise_with(stream_key, dims, spread, most, cuts, heavy, kind=jnp.bfloat16):
    array = spread * jax.random.normal(stream_key, dims, jnp.float32)
    if cuts:
        array = array * level_of(stream_key, dims, cuts, -0.22, 0.18)
    return jnp.clip(raised(array, jax.random.fold_in(stream_key, 3), *heavy), -most, most).astype(kind)


def setup_inputs(seed: int = 0) -> dict:
    key_list = jax.random.split(jax.random.key(seed), 9)
    return {
        "query_rows": draw_query_rows(jax.random.fold_in(key_list[8], 71), 0),
        "key_rows": draw_key_rows(jax.random.fold_in(key_list[8], 71), 0),
        "value_rows": scatter_about(key_list[2], (SAMPLES, SEQ, FEAT), 1.0, 6.0, ((0, 16), (1, 8))),
        "attention_out": noise_with(key_list[3], (SAMPLES, SEQ, FEAT), 1.0, 6.0, ((0, 16), (1, 8)), (0, 2, 16, 2.0)),
        "output_grad": scatter_about(key_list[4], (SAMPLES, SEQ, D), 1.0, 6.0, ((0, 16), (1, 8))),
        "output_weight": scatter_about(key_list[5], (FEAT, D), FEAT ** -0.5, 0.15625, ((0, 16),)),
        "tile_mask": draw_tile_mask(jax.random.fold_in(key_list[8], 71), 0),
        "live_tiles": draw_live_tiles(jax.random.fold_in(key_list[8], 71), 0),
    }


MASKED_SCORE = -1e+30

def rounded(values):
    return lax.optimization_barrier(values.astype(jnp.bfloat16)).astype(jnp.float32)

def tile_backward(query_tile, back_tile, output_tile, key_block, value_block, allowed, scaling):
    query_wide = query_tile.astype(jnp.float32)
    back_wide = back_tile.astype(jnp.float32)
    output_wide = output_tile.astype(jnp.float32)
    key_wide = key_block.astype(jnp.float32)
    value_wide = value_block.astype(jnp.float32)
    scores = jnp.einsum('qhd,khd->hqk', query_wide, key_wide) * scaling
    scores = jnp.where(allowed[None, None, :], scores, MASKED_SCORE)
    highest = lax.optimization_barrier(jnp.max(scores, axis=2, keepdims=True))
    weights = jnp.where(allowed[None, None, :], jnp.exp(scores - highest), 0.0)
    totals = jnp.maximum(lax.optimization_barrier(jnp.sum(weights, axis=2, keepdims=True)), 1.0)
    attention_weights = weights / totals
    weights_low = rounded(attention_weights)
    row_dots = jnp.einsum('qhd,qhd->hq', back_wide, output_wide)
    grad_weights = jnp.einsum('qhd,khd->hqk', back_wide, value_wide)
    grad_scores = rounded(attention_weights * (grad_weights - row_dots[:, :, None]) * scaling)
    query_part = jnp.einsum('hqk,khd->qhd', grad_scores, key_wide)
    key_part = jnp.einsum('hqk,qhd->khd', grad_scores, query_wide)
    value_part = jnp.einsum('hqk,qhd->khd', weights_low, back_wide)
    return (query_part, key_part, value_part)

def combine_terms(shares, tiles):
    own_term = shares[:, 1]
    zero_tile = jnp.zeros_like(shares[:1, 0])
    from_next = jnp.concatenate([shares[1:, 0], zero_tile], 0)
    from_prev = jnp.concatenate([zero_tile, shares[:-1, 2]], 0)
    tile_ids = jnp.arange(tiles, dtype=jnp.int32)
    next_cross = ((tile_ids + 1) % TT_DEV == 0)[:, None, None, None]
    prev_cross = (tile_ids % TT_DEV == 0)[:, None, None, None]
    from_next = jnp.where(next_cross, rounded(from_next), from_next)
    from_prev = jnp.where(prev_cross, rounded(from_prev), from_prev)
    return (own_term + from_next + from_prev).astype(jnp.bfloat16)

def sample_backward(query_one, key_one, value_one, output_one, grad_one, output_weight, mask_one, count_one):
    tiles = query_one.shape[0] // TILE
    num_heads = query_one.shape[1] // HDIM
    scaling = 1.0 / math.sqrt(HDIM)
    out_back = jnp.dot(grad_one, output_weight.T, preferred_element_type=jnp.float32).astype(jnp.bfloat16)

    def as_tiles(values):
        return values.reshape(tiles, TILE, num_heads, HDIM)
    query_tiles = as_tiles(query_one)
    back_tiles = as_tiles(out_back)
    output_tiles = as_tiles(output_one)
    padding = jnp.zeros((1, TILE, num_heads, HDIM), jnp.bfloat16)
    key_padded = jnp.concatenate([padding, as_tiles(key_one), padding], 0)
    value_padded = jnp.concatenate([padding, as_tiles(value_one), padding], 0)
    tile_ids = jnp.arange(tiles, dtype=jnp.int32)
    tile_live = tile_ids % TT_DEV < count_one[tile_ids // TT_DEV]
    dead_edge = jnp.zeros((1,), jnp.bool_)
    live_padded = jnp.concatenate([dead_edge, tile_live, dead_edge], 0)

    def per_tile(tile_id):
        key_block = lax.dynamic_slice_in_dim(key_padded, tile_id, 3, 0).reshape(3 * TILE, num_heads, HDIM)
        value_block = lax.dynamic_slice_in_dim(value_padded, tile_id, 3, 0).reshape(3 * TILE, num_heads, HDIM)
        near_live = lax.dynamic_slice_in_dim(live_padded, tile_id, 3, 0)
        allowed_tiles = (mask_one[tile_id] == 1) & near_live & tile_live[tile_id]
        allowed = jnp.repeat(allowed_tiles, TILE)
        query_part, key_part, value_part = tile_backward(query_tiles[tile_id], back_tiles[tile_id], output_tiles[tile_id], key_block, value_block, allowed, scaling)
        return (query_part.astype(jnp.bfloat16), key_part.reshape(3, TILE, num_heads, HDIM), value_part.reshape(3, TILE, num_heads, HDIM))
    query_grad, key_shares, value_shares = lax.map(per_tile, tile_ids)
    features = query_one.shape[1]
    key_grad = combine_terms(key_shares, tiles)
    value_grad = combine_terms(value_shares, tiles)
    return (query_grad.reshape(tiles * TILE, features), key_grad.reshape(tiles * TILE, features), value_grad.reshape(tiles * TILE, features))

def reference(query_rows, key_rows, value_rows, attention_out, output_grad, output_weight, tile_mask, live_tiles):

    def scan_step(grad_total, sample_items):
        query_one, key_one, value_one, output_one, grad_one, mask_one, count_one = sample_items
        sample_grads = sample_backward(query_one, key_one, value_one, output_one, grad_one, output_weight, mask_one, count_one)
        weight_term = lax.dot_general(output_one, grad_one, (((0,), (0,)), ((), ())), preferred_element_type=jnp.float32)
        return (grad_total + weight_term, sample_grads)
    initial = jnp.zeros((FEAT, D), jnp.float32)
    grad_total, sample_grads = lax.scan(scan_step, initial, (query_rows, key_rows, value_rows, attention_out, output_grad, tile_mask, live_tiles))
    weight_grad = grad_total / math.sqrt(SAMPLES * SEQ)
    return (sample_grads[0], sample_grads[1], sample_grads[2], weight_grad)
```

```python
import functools
import math

import jax
import jax.numpy as jnp
from jax import lax
from jax.experimental import pallas as pl
from jax.experimental.pallas import tpu as pltpu
from jax.sharding import PartitionSpec as P

HDIM = 128
TILE = 384
SLAB = 768
FEAT = 1536
WIDTH = 3072
GROUP = 3
BLOCK = GROUP * HDIM
QUARTER = WIDTH // 4
ROWS = 96
AXES = ("seq", "dp")
SCALE = 1.0 / math.sqrt(HDIM)
SCALE2 = SCALE / math.log(2.0)
NEVER = 1e30
LIMIT = 48 * 1024 * 1024
F32 = jnp.float32
BF16 = jnp.bfloat16


def place(z, y, x, core):
    return ((z % 4) * 2 + (x % 4) // 2) * 16 + (y % 4) * 4 + (x % 2) * 2 + core


def route(target):
    pairs = []
    for z in range(4):
        for y in range(4):
            for x in range(4):
                for core in range(2):
                    to = target(z, y, x, core)
                    if to is not None:
                        pairs.append((place(z, y, x, core), place(*to)))
    return pairs


def slab_step(step):
    def target(z, y, x, core):
        slab = z * 2 + x // 2 + step
        if slab < 0 or slab > 7:
            return None
        return (slab // 2, y, (slab % 2) * 2 + x % 2, core)

    return route(target)


UP = slab_step(1)
DOWN = slab_step(-1)
SWAP_LOW = route(lambda z, y, x, core: (z, y, x ^ 1, core))
SWAP_HIGH = route(lambda z, y, x, core: (z, y, x ^ 2, core))
SWAP_CORE = route(lambda z, y, x, core: (z, y, x, 1 - core))


def from_first(step):
    return route(
        lambda z, y, x, core: (z, y - step, x, core) if core == 0 else (z - step, y, x, core)
    )


def from_second(step):
    return route(
        lambda z, y, x, core: (z - step, y, x, core) if core == 0 else (z, y - step, x, core)
    )


def send(block, pairs):
    return lax.ppermute(block, AXES, pairs)


def dot(a, b, dims):
    return lax.dot_general(a, b, (dims, ((), ())), preferred_element_type=F32)


NT = ((1,), (1,))
NN = ((1,), (0,))
TN = ((0,), (0,))


def params(**kwargs):
    return pltpu.CompilerParams(vmem_limit_bytes=LIMIT, **kwargs)


def cost(flops, moved, exps=0):
    return pl.CostEstimate(flops=int(flops), bytes_accessed=int(moved), transcendentals=int(exps))


def head_of(dy, j, where):
    return lax.rem(where[0] + dy, 4) * GROUP + j


def own_stats_kernel(where, q, k, bias, out):
    queries = q[...]
    first = dot(k[:TILE], queries, NT) * SCALE2 + bias[0:1]
    second = dot(k[TILE:], queries, NT) * SCALE2 + bias[1:2]
    highest = jnp.maximum(
        jnp.max(first, axis=0, keepdims=True), jnp.max(second, axis=0, keepdims=True)
    )
    total = jnp.sum(jnp.exp2(first - highest), axis=0, keepdims=True) + jnp.sum(
        jnp.exp2(second - highest), axis=0, keepdims=True
    )
    out[0] = highest + jnp.log2(total)


def own_stats(where, q, k, bias):
    return pl.pallas_call(
        own_stats_kernel,
        grid_spec=pltpu.PrefetchScalarGridSpec(
            num_scalar_prefetch=1,
            grid=(4, GROUP),
            in_specs=[
                pl.BlockSpec((SLAB, HDIM), lambda d, j, w: (0, head_of(d, j, w))),
                pl.BlockSpec((SLAB, HDIM), lambda d, j, w: (0, head_of(d, j, w))),
                pl.BlockSpec((2, SLAB), lambda d, j, w: (0, 0)),
            ],
            out_specs=pl.BlockSpec((1, 1, SLAB), lambda d, j, w: (d * GROUP + j, 0, 0)),
        ),
        out_shape=jax.ShapeDtypeStruct((12, 1, SLAB), F32),
        compiler_params=params(),
        cost_estimate=cost(2 * SLAB * SLAB * FEAT, 5e6, 12 * SLAB * SLAB),
        name="own_stats",
    )(where, q, k, bias)


def far_stats_kernel(where, qb, qa, k, out_b, out_a):
    for queries, keys, out in ((qb, k[:TILE], out_b), (qa, k[TILE:], out_a)):
        scores = dot(keys, queries[...], NT) * SCALE2
        highest = jnp.max(scores, axis=0, keepdims=True)
        total = jnp.sum(jnp.exp2(scores - highest), axis=0, keepdims=True)
        out[0] = highest + jnp.log2(total)


def far_stats(where, qb, qa, k):
    half = pl.BlockSpec((TILE, HDIM), lambda d, j, w: (0, head_of(d, j, w)))
    row = pl.BlockSpec((1, 1, TILE), lambda d, j, w: (d * GROUP + j, 0, 0))
    return pl.pallas_call(
        far_stats_kernel,
        grid_spec=pltpu.PrefetchScalarGridSpec(
            num_scalar_prefetch=1,
            grid=(4, GROUP),
            in_specs=[
                half,
                half,
                pl.BlockSpec((SLAB, HDIM), lambda d, j, w: (0, head_of(d, j, w))),
            ],
            out_specs=[row, row],
        ),
        out_shape=[jax.ShapeDtypeStruct((12, 1, TILE), F32)] * 2,
        compiler_params=params(),
        cost_estimate=cost(SLAB * SLAB * FEAT, 5e6, 6 * SLAB * SLAB),
        name="far_stats",
    )(where, qb, qa, k)


def back_kernel(where, g, mine, other, o, up, down, dots, total, weight):
    dz = pl.program_id(1)

    @pl.when(where[2] == 0)
    def _():
        for low in range(2):
            weight[pl.ds(low * 192, ROWS)] = mine[0, 0, low]
            weight[pl.ds(low * 192 + ROWS, ROWS)] = other[0, 0, low]

    @pl.when(where[2] == 1)
    def _():
        for low in range(2):
            weight[pl.ds(low * 192, ROWS)] = other[0, 0, low]
            weight[pl.ds(low * 192 + ROWS, ROWS)] = mine[0, 0, low]

    product = dot(g[...], weight[...], NT)

    @pl.when(dz == 0)
    def _():
        total[...] = product

    @pl.when(dz > 0)
    def _():
        total[...] += product

    @pl.when(dz == 3)
    def _():
        ones = jnp.ones((8, HDIM), BF16)
        for j in range(GROUP):
            columns = slice(j * HDIM, (j + 1) * HDIM)
            back = total[:, columns].astype(BF16)
            down[0, :, columns] = back[:TILE]
            up[0, :, columns] = back[TILE:]
            products = back.astype(F32) * o[:, columns].astype(F32)
            coarse = products.astype(BF16)
            fine = (products - coarse.astype(F32)).astype(BF16)
            dots[0, j] = (dot(ones, coarse, NT) + dot(ones, fine, NT))[0:1]


def back(where, g, mine, other, o, dy0, count):
    def straight(d, e, w):
        return jnp.where(w[2] == 0, e, dy0 + d), jnp.where(w[2] == 0, dy0 + d, e)

    def crossed(d, e, w):
        return jnp.where(w[2] == 0, dy0 + d, e), jnp.where(w[2] == 0, e, dy0 + d)

    piece = (1, 1, 2, ROWS, QUARTER)
    half = pl.BlockSpec((1, TILE, BLOCK), lambda d, e, w: (d, 0, 0))
    return pl.pallas_call(
        back_kernel,
        grid_spec=pltpu.PrefetchScalarGridSpec(
            num_scalar_prefetch=1,
            grid=(count, 4),
            in_specs=[
                pl.BlockSpec((SLAB, QUARTER), lambda d, e, w: (0, lax.rem(w[1] + e, 4))),
                pl.BlockSpec(piece, lambda d, e, w: straight(d, e, w) + (0, 0, 0)),
                pl.BlockSpec(piece, lambda d, e, w: crossed(d, e, w) + (0, 0, 0)),
                pl.BlockSpec((SLAB, BLOCK), lambda d, e, w: (0, lax.rem(w[0] + dy0 + d, 4))),
            ],
            out_specs=[
                half,
                half,
                pl.BlockSpec((1, GROUP, 1, SLAB), lambda d, e, w: (d, 0, 0, 0)),
            ],
            scratch_shapes=[pltpu.VMEM((SLAB, BLOCK), F32), pltpu.VMEM((BLOCK, QUARTER), BF16)],
        ),
        out_shape=[
            jax.ShapeDtypeStruct((count, TILE, BLOCK), BF16),
            jax.ShapeDtypeStruct((count, TILE, BLOCK), BF16),
            jax.ShapeDtypeStruct((count, GROUP, 1, SLAB), F32),
        ],
        compiler_params=params(),
        cost_estimate=cost(count * 2 * SLAB * BLOCK * WIDTH, count * 9e6),
        name="out_back",
    )(where, g, mine, other, o)


def own_kernel(where, q, k, v, up, down, rows, dots, dq, dk, dv):
    queries = q[...]
    backs = jnp.concatenate([down[0], up[0]], axis=0)
    row_dots = dots[0, 0]
    query_total = None
    for tile in range(2):
        part = slice(tile * TILE, (tile + 1) * TILE)
        keys = k[part]
        weights = jnp.exp2(dot(keys, queries, NT) * SCALE2 - rows[0, tile : tile + 1])
        grads = (weights * (dot(v[part], backs, NT) - row_dots)).astype(BF16)
        dv[0, part] = dot(weights.astype(BF16), backs, NN)
        dk[0, part] = dot(grads, queries, NN) * SCALE
        share = dot(grads, keys, TN)
        query_total = share if query_total is None else query_total + share
    dq[0] = query_total * SCALE


def own_grads(where, q, k, v, up, down, rows, dots, dy0, count):
    full = pl.BlockSpec((SLAB, HDIM), lambda d, j, w: (0, head_of(dy0 + d, j, w)))
    half = pl.BlockSpec((1, TILE, HDIM), lambda d, j, w: (d, 0, j))
    result = pl.BlockSpec((1, SLAB, HDIM), lambda d, j, w: (d, 0, j))
    return pl.pallas_call(
        own_kernel,
        grid_spec=pltpu.PrefetchScalarGridSpec(
            num_scalar_prefetch=1,
            grid=(count, GROUP),
            in_specs=[
                full,
                full,
                full,
                half,
                half,
                pl.BlockSpec((1, 2, SLAB), lambda d, j, w: ((dy0 + d) * GROUP + j, 0, 0)),
                pl.BlockSpec((1, 1, 1, SLAB), lambda d, j, w: (d, j, 0, 0)),
            ],
            out_specs=[result] * 3,
        ),
        out_shape=[jax.ShapeDtypeStruct((count, SLAB, BLOCK), F32)] * 3,
        compiler_params=params(),
        cost_estimate=cost(
            count * GROUP * 10 * SLAB * SLAB * HDIM, count * 7e6, count * GROUP * SLAB * SLAB
        ),
        name="own_grads",
    )(where, q, k, v, up, down, rows, dots)


def far_kernel(
    where, qb, qa, backb, backa, rowb, rowa, k, v, dk_own, dv_own, *rest
):
    dqb, dqa, dk, dv = rest[-4:]
    sides = ((qb, backb, rowb, dqb), (qa, backa, rowa, dqa))
    for tile, (q, b, row, dq) in enumerate(sides):
        part = slice(tile * TILE, (tile + 1) * TILE)
        keys = k[part]
        queries = q[...]
        backs = b[0]
        weights = jnp.exp2(dot(keys, queries, NT) * SCALE2 - row[0, 0:1])
        grads = (weights * (dot(v[part], backs, NT) - row[0, 1:2])).astype(BF16)
        dq[0] = (dot(grads, keys, TN) * SCALE).astype(BF16)
        dk[part] = (dk_own[0, part] + dot(grads, queries, NN) * SCALE).astype(BF16)
        dv[part] = (dv_own[0, part] + dot(weights.astype(BF16), backs, NN)).astype(BF16)


def far_grads(where, qb, qa, backb, backa, rowb, rowa, k, v, dk_own, dv_own, held, dy0, count):
    full = pl.BlockSpec((SLAB, HDIM), lambda d, j, w: (0, head_of(dy0 + d, j, w)))
    edge = pl.BlockSpec((TILE, HDIM), lambda d, j, w: (0, head_of(dy0 + d, j, w)))
    half = pl.BlockSpec((1, TILE, HDIM), lambda d, j, w: (d, 0, j))
    own = pl.BlockSpec((1, SLAB, HDIM), lambda d, j, w: (d, 0, j))
    row = pl.BlockSpec((1, 2, TILE), lambda d, j, w: ((dy0 + d) * GROUP + j, 0, 0))
    aliases = {11: 2, 12: 3} if held else {}
    return pl.pallas_call(
        far_kernel,
        grid_spec=pltpu.PrefetchScalarGridSpec(
            num_scalar_prefetch=1,
            grid=(count, GROUP),
            in_specs=[edge, edge, half, half, row, row, full, full, own, own]
            + [pl.BlockSpec(memory_space=pl.ANY)] * len(held),
            out_specs=[half, half, full, full],
        ),
        out_shape=[jax.ShapeDtypeStruct((count, TILE, BLOCK), BF16)] * 2
        + [jax.ShapeDtypeStruct((SLAB, FEAT), BF16)] * 2,
        input_output_aliases=aliases,
        compiler_params=params(),
        cost_estimate=cost(
            count * GROUP * 5 * SLAB * SLAB * HDIM, count * 6e6, count * GROUP * SLAB * TILE
        ),
        name="far_grads",
    )(where, qb, qa, backb, backa, rowb, rowa, k, v, dk_own, dv_own, *held)


def join_kernel(where, own, low, high, *rest):
    out = rest[-1]
    out[:TILE] = (own[0, :TILE] + low[0].astype(F32)).astype(BF16)
    out[TILE:] = (own[0, TILE:] + high[0].astype(F32)).astype(BF16)


def join(where, own, low, high, held, dy0, count):
    half = pl.BlockSpec((1, TILE, BLOCK), lambda d, w: (d, 0, 0))
    return pl.pallas_call(
        join_kernel,
        grid_spec=pltpu.PrefetchScalarGridSpec(
            num_scalar_prefetch=1,
            grid=(count,),
            in_specs=[pl.BlockSpec((1, SLAB, BLOCK), lambda d, w: (d, 0, 0)), half, half]
            + [pl.BlockSpec(memory_space=pl.ANY)] * len(held),
            out_specs=pl.BlockSpec((SLAB, BLOCK), lambda d, w: (0, lax.rem(w[0] + dy0 + d, 4))),
        ),
        out_shape=jax.ShapeDtypeStruct((SLAB, FEAT), BF16),
        input_output_aliases={4: 0} if held else {},
        compiler_params=params(),
        cost_estimate=cost(count * SLAB * BLOCK, count * 3e6),
        name="join_query_grad",
    )(where, own, low, high, *held)


def weight_term_kernel(o, g, out):
    product = dot(o[...], g[...], TN).astype(BF16)
    for low in range(2):
        for core in range(2):
            start = (low * 2 + core) * ROWS
            out[0, core, 0, low] = product[start : start + ROWS]


def weight_term(o, g):
    return pl.pallas_call(
        weight_term_kernel,
        grid=(4, 4),
        in_specs=[
            pl.BlockSpec((SLAB, BLOCK), lambda y, z: (0, y)),
            pl.BlockSpec((SLAB, QUARTER), lambda y, z: (0, z)),
        ],
        out_specs=pl.BlockSpec((1, 2, 1, 2, ROWS, QUARTER), lambda y, z: (y, 0, z, 0, 0, 0)),
        out_shape=jax.ShapeDtypeStruct((4, 2, 4, 2, ROWS, QUARTER), BF16),
        compiler_params=params(),
        cost_estimate=cost(2 * SLAB * FEAT * WIDTH, 3.5e7),
        name="weight_term",
    )(o, g)


def gather_weight(weight, z, low):
    quarter = lax.dynamic_slice(weight, (0, z * QUARTER), (ROWS, QUARTER))
    partner = send(quarter, SWAP_LOW)
    pair = jnp.where(
        low == 0, jnp.stack([quarter, partner]), jnp.stack([partner, quarter])
    )
    line = jnp.stack([pair] + [send(pair, from_first(step)) for step in (1, 2, 3)])
    plane = jnp.stack([line] + [send(line, from_second(step)) for step in (1, 2, 3)])
    return plane, send(plane, SWAP_CORE)


def weight_gradient(term, z, low, normaliser):
    groups = [
        [place(z, y, x, core) for y in range(4) for core in range(2) for z in range(4)]
        for x in range(4)
    ]
    part = lax.psum_scatter(
        term.reshape(32 * 2 * ROWS, QUARTER),
        AXES,
        scatter_dimension=0,
        axis_index_groups=groups,
        tiled=True,
    ).reshape(2, ROWS, QUARTER)
    kept = jnp.where(low == 0, part[0], part[1]).astype(F32)
    given = jnp.where(low == 0, part[1], part[0])
    both = (kept + send(given, SWAP_LOW).astype(F32)).astype(BF16)
    whole = both.astype(F32) + send(both, SWAP_HIGH).astype(F32)
    lines = [
        [place(z, y, x, core) for z in range(4)]
        for y in range(4)
        for x in range(4)
        for core in range(2)
    ]
    return lax.all_gather(
        whole * normaliser, AXES, axis=1, axis_index_groups=lines, tiled=True
    )


RUNS = ((0, 2), (2, 2))


def body(
    query_rows,
    key_rows,
    value_rows,
    attention_out,
    output_grad,
    output_weight,
    tile_mask,
    live_tiles,
):
    q, k, v, o, g = (
        a[0] for a in (query_rows, key_rows, value_rows, attention_out, output_grad)
    )
    slab = lax.axis_index("seq")
    row = lax.axis_index("dp")
    z = slab // 2
    y = row // 4
    low = (row // 2) % 2
    core = row % 2
    where = jnp.stack([y, z, core]).astype(jnp.int32)

    q_below = send(q[TILE:], UP)
    q_above = send(q[:TILE], DOWN)
    mine, other = gather_weight(output_weight, z, low)

    counts = live_tiles[0]
    slabs = jnp.arange(8, dtype=jnp.int32)

    def live(which, tile):
        return jnp.any((slabs == which) & (counts > tile))

    lives = [live(slab - 1, 1), live(slab, 0), live(slab, 1), live(slab + 1, 0)]
    marks = tile_mask[0] == 1
    allowed = [
        [marks[a, b] & lives[a + 1] & lives[a + b] for b in range(3)] for a in range(2)
    ]

    def by_query(first, second):
        return jnp.concatenate(
            [jnp.broadcast_to(first, (1, TILE)), jnp.broadcast_to(second, (1, TILE))], axis=1
        )

    own_allowed = [by_query(allowed[0][1], allowed[1][0]), by_query(allowed[0][2], allowed[1][1])]
    far_allowed = by_query(allowed[0][0], allowed[1][2])
    bias = jnp.where(jnp.concatenate(own_allowed, axis=0), 0.0, -NEVER).astype(F32)

    own_row = own_stats(where, q, k, bias)
    stat_b, stat_a = far_stats(where, q_below, q_above, k)
    far_row = jnp.concatenate([send(stat_a, UP), send(stat_b, DOWN)], axis=2)
    far_row = jnp.where(far_allowed[None], far_row, -NEVER)
    top = jnp.maximum(own_row, far_row)
    row_total = top + jnp.log2(jnp.exp2(own_row - top) + jnp.exp2(far_row - top))
    own_rows = jnp.concatenate(
        [jnp.where(a[None], row_total, NEVER) for a in own_allowed], axis=1
    )
    far_rows = jnp.where(far_allowed[None], row_total, NEVER)

    backs = [back(where, g, mine, other, o, *run) for run in RUNS]
    dots = jnp.concatenate([b[2] for b in backs], axis=0).reshape(12, 1, SLAB)
    message = jnp.concatenate([far_rows, dots], axis=1)
    row_b = send(message[:, :, TILE:], UP)
    row_a = send(message[:, :, :TILE], DOWN)
    row_b = jnp.where(slab == 0, NEVER, row_b)
    row_a = jnp.where(slab == 7, NEVER, row_a)

    back_b = [send(b[0], UP) for b in backs]
    back_a = [send(b[1], DOWN) for b in backs]

    term = weight_term(o, g)
    weight_grad = weight_gradient(term, z, low, 1.0 / math.sqrt(16 * 6144))

    held = ()
    joined = ()
    finished = []
    for index, (dy0, count) in enumerate(RUNS):
        up, down, own_dots = backs[index]
        dq, dk, dv = own_grads(where, q, k, v, up, down, own_rows, own_dots, dy0, count)
        dqb, dqa, *held = far_grads(
            where,
            q_below,
            q_above,
            back_b[index],
            back_a[index],
            row_b,
            row_a,
            k,
            v,
            dk,
            dv,
            tuple(held),
            dy0,
            count,
        )
        finished.append((dq, send(dqa, UP), send(dqb, DOWN), dy0, count))
    for dq, from_below, from_above, dy0, count in finished:
        joined = (join(where, dq, from_below, from_above, joined, dy0, count),)
    return joined[0][None], held[0][None], held[1][None], weight_grad


def solution(mesh):
    in_specs = (
        P("dp", "seq", None),
        P("dp", "seq", None),
        P("dp", "seq", None),
        P("dp", "seq", None),
        P("dp", "seq", None),
        P("dp", None),
        P("dp", "seq", None),
        P("dp", None),
    )
    out_specs = (P("dp", "seq", None), P("dp", "seq", None), P("dp", "seq", None), P("dp", None))
    return jax.shard_map(body, mesh=mesh, in_specs=in_specs, out_specs=out_specs, check_vma=False)
```

```python
import functools
import math

import jax
import jax.numpy as jnp
from jax import lax
from jax.experimental import pallas as pl
from jax.experimental.pallas import tpu as pltpu
from jax.sharding import PartitionSpec as P

HDIM = 128
TILE = 384
SLAB = 768
FEAT = 1536
WIDTH = 3072
GROUP = 3
BLOCK = GROUP * HDIM
QUARTER = WIDTH // 4
ROWS = 96
AXES = ("seq", "dp")
SCALE = 1.0 / math.sqrt(HDIM)
SCALE2 = SCALE / math.log(2.0)
NEVER = 1e30
EXTRA = 16
LIMIT = 48 * 1024 * 1024
F32 = jnp.float32
BF16 = jnp.bfloat16


def place(z, y, x, core):
    return ((z % 4) * 2 + (x % 4) // 2) * 16 + (y % 4) * 4 + (x % 2) * 2 + core


def route(target):
    pairs = []
    for z in range(4):
        for y in range(4):
            for x in range(4):
                for core in range(2):
                    to = target(z, y, x, core)
                    if to is not None:
                        pairs.append((place(z, y, x, core), place(*to)))
    return pairs


def slab_step(step):
    def target(z, y, x, core):
        slab = z * 2 + x // 2 + step
        if slab < 0 or slab > 7:
            return None
        return (slab // 2, y, (slab % 2) * 2 + x % 2, core)

    return route(target)


UP = slab_step(1)
DOWN = slab_step(-1)
CORES = [frozenset(place(z, y, x, core) for z in range(4) for y in range(4) for x in range(4)) for core in range(2)]
ROUTE_A = [p for p in UP if p[0] in CORES[0]] + [p for p in DOWN if p[0] in CORES[1]]
ROUTE_B = [p for p in DOWN if p[0] in CORES[0]] + [p for p in UP if p[0] in CORES[1]]
SWAP_LOW = route(lambda z, y, x, core: (z, y, x ^ 1, core))
SWAP_HIGH = route(lambda z, y, x, core: (z, y, x ^ 2, core))
SWAP_CORE = route(lambda z, y, x, core: (z, y, x, 1 - core))


def from_along_z(step):
    return route(lambda z, y, x, core: (z - step, y, x, core))


def swap_first(bit):
    return route(
        lambda z, y, x, core: (z, y ^ bit, x, core) if core == 0 else (z ^ bit, y, x, core)
    )


def swap_second(bit):
    return route(
        lambda z, y, x, core: (z ^ bit, y, x, core) if core == 0 else (z, y ^ bit, x, core)
    )


def from_first(step):
    return route(
        lambda z, y, x, core: (z, y - step, x, core) if core == 0 else (z - step, y, x, core)
    )


def from_second(step):
    return route(
        lambda z, y, x, core: (z - step, y, x, core) if core == 0 else (z, y - step, x, core)
    )


def send(block, pairs):
    return lax.ppermute(block, AXES, pairs)


def dot(a, b, dims):
    return lax.dot_general(a, b, (dims, ((), ())), preferred_element_type=F32)


NT = ((1,), (1,))
NN = ((1,), (0,))
TN = ((0,), (0,))


def params(**kwargs):
    return pltpu.CompilerParams(vmem_limit_bytes=LIMIT, **kwargs)


HIDES = pl.CostEstimate(flops=100_000_000_000, bytes_accessed=1_000_000, transcendentals=0)
STEP = pl.CostEstimate(flops=100_000_000, bytes_accessed=100_000, transcendentals=0)


def columns(j):
    return slice(j * HDIM, (j + 1) * HDIM)


def first_tile(where):
    return pl.multiple_of((1 - where[2]) * TILE, TILE)


def second_tile(where):
    return pl.multiple_of(where[2] * TILE, TILE)


def own_stats_kernel(where, q, k, bias, out):
    for j in range(GROUP):
        keys = k[:, columns(j)]
        queries = jnp.concatenate(
            [q[pl.ds(start(where), TILE), columns(j)] for start in (first_tile, second_tile)], axis=0
        )
        first = dot(keys[:TILE], queries, NT) * SCALE2 + bias[0:1]
        second = dot(keys[TILE:], queries, NT) * SCALE2 + bias[1:2]
        highest = jnp.maximum(
            jnp.max(first, axis=0, keepdims=True), jnp.max(second, axis=0, keepdims=True)
        )
        total = jnp.sum(jnp.exp2(first - highest), axis=0, keepdims=True) + jnp.sum(
            jnp.exp2(second - highest), axis=0, keepdims=True
        )
        out[j] = highest + jnp.log2(total)


def own_stats(where, q, k, bias):
    wide = pl.BlockSpec((SLAB, BLOCK), lambda d, w: (0, lax.rem(w[0] + d, 4)))
    return pl.pallas_call(
        own_stats_kernel,
        grid_spec=pltpu.PrefetchScalarGridSpec(
            num_scalar_prefetch=1,
            grid=(4,),
            in_specs=[wide, wide, pl.BlockSpec((2, SLAB), lambda d, w: (0, 0))],
            out_specs=pl.BlockSpec((GROUP, 1, SLAB), lambda d, w: (d, 0, 0)),
        ),
        out_shape=jax.ShapeDtypeStruct((12, 1, SLAB), F32),
        compiler_params=params(),
        cost_estimate=STEP,
        name="own_stats",
    )(where, q, k, bias)


def far_stats_kernel(where, q, k, out):
    for j in range(GROUP):
        scores = dot(k[:, columns(j)], q[0, :, columns(j)], NT) * SCALE2
        highest = jnp.max(scores, axis=0, keepdims=True)
        total = jnp.sum(jnp.exp2(scores - highest), axis=0, keepdims=True)
        out[j] = highest + jnp.log2(total)


def key_tile(side, w):
    return w[2] if side == 0 else 1 - w[2]


def far_stats(where, side, q, k):
    return pl.pallas_call(
        far_stats_kernel,
        grid_spec=pltpu.PrefetchScalarGridSpec(
            num_scalar_prefetch=1,
            grid=(4,),
            in_specs=[
                pl.BlockSpec((1, TILE, BLOCK), lambda d, w: (d, 0, 0)),
                pl.BlockSpec((TILE, BLOCK), lambda d, w: (key_tile(side, w), lax.rem(w[0] + d, 4))),
            ],
            out_specs=pl.BlockSpec((GROUP, 1, TILE), lambda d, w: (d, 0, 0)),
        ),
        out_shape=jax.ShapeDtypeStruct((12, 1, TILE), F32),
        compiler_params=params(),
        cost_estimate=STEP,
        name="far_stats",
    )(where, q, k)


def back_kernel(where, g, mine_z, mine_y, other_z, other_y, o, back, dots, weight):
    for core in range(2):

        @pl.when(where[2] == core)
        def _():
            for dz in range(4):
                block = pl.ds(pl.multiple_of(lax.rem(where[1] + dz, 4) * QUARTER, QUARTER), QUARTER)
                for low in range(2):
                    for holder in range(2):
                        if core == holder:
                            piece = mine_z[dz, 0, low] if core == 0 else mine_y[0, dz, low]
                        else:
                            piece = other_y[0, dz, low] if core == 0 else other_z[dz, 0, low]
                        weight[pl.ds((low * 2 + holder) * ROWS, ROWS), block] = piece

    result = dot(g[...], weight[...], NT).astype(BF16)
    back[0, :TILE] = result
    back[0, TILE:] = jnp.zeros((EXTRA, BLOCK), BF16)
    products = result.astype(F32) * o[...].astype(F32)
    coarse = products.astype(BF16)
    fine = (products - coarse.astype(F32)).astype(BF16)
    ones = jnp.ones((8, HDIM), BF16)
    for j in range(GROUP):
        summed = dot(ones, coarse[:, columns(j)], NT) + dot(ones, fine[:, columns(j)], NT)
        dots[j] = summed[0:1]


def back(where, side, g, mine, other, o):
    def tile(w):
        return 1 - w[2] if side == 0 else w[2]

    along_z = pl.BlockSpec((4, 1, 2, ROWS, QUARTER), lambda d, w: (0, d, 0, 0, 0))
    along_y = pl.BlockSpec((1, 4, 2, ROWS, QUARTER), lambda d, w: (d, 0, 0, 0, 0))
    return pl.pallas_call(
        back_kernel,
        grid_spec=pltpu.PrefetchScalarGridSpec(
            num_scalar_prefetch=1,
            grid=(4,),
            in_specs=[
                pl.BlockSpec((TILE, WIDTH), lambda d, w: (tile(w), 0)),
                along_z,
                along_y,
                along_z,
                along_y,
                pl.BlockSpec((TILE, BLOCK), lambda d, w: (tile(w), lax.rem(w[0] + d, 4))),
            ],
            out_specs=[
                pl.BlockSpec((1, TILE + EXTRA, BLOCK), lambda d, w: (d, 0, 0)),
                pl.BlockSpec((GROUP, 1, TILE), lambda d, w: (d, 0, 0)),
            ],
            scratch_shapes=[pltpu.VMEM((BLOCK, WIDTH), BF16)],
        ),
        out_shape=[
            jax.ShapeDtypeStruct((4, TILE + EXTRA, BLOCK), BF16),
            jax.ShapeDtypeStruct((12, 1, TILE), F32),
        ],
        compiler_params=params(),
        cost_estimate=HIDES,
        name="out_back",
    )(where, g, mine, mine, other, other, o)


def pieces(value, count):
    parts = []
    for _ in range(count):
        part = lax.reduce_precision(value, exponent_bits=8, mantissa_bits=7)
        parts.append(part.astype(BF16))
        value = value - part
    return parts


def with_statistics(block, row, dots):
    parts = jnp.concatenate(pieces(row, 3) + pieces(dots, 2), axis=1)
    parts = parts.reshape(4, GROUP * 5, TILE)
    return lax.dynamic_update_slice(block, parts, (0, TILE, 0))


def own_kernel(where, q, k, v, back_a, back_b, rows, dots_a, dots_b, dk_a, dv_a, dk_b, dv_b, *rest):
    dq, dk, dv = rest[-3:]
    for j in range(GROUP):
        head = columns(j)
        queries = jnp.concatenate(
            [q[pl.ds(start(where), TILE), head] for start in (first_tile, second_tile)], axis=0
        )
        backs = jnp.concatenate([back_a[0, :TILE, head], back_b[0, :TILE, head]], axis=0)
        dots = jnp.concatenate([dots_a[j], dots_b[j]], axis=1)
        query_total = None
        sides = ((second_tile, dk_a, dv_a), (first_tile, dk_b, dv_b))
        for side, (start, dk_far, dv_far) in enumerate(sides):
            part = pl.ds(start(where), TILE)
            keys = k[part, head]
            weights = jnp.exp2(dot(keys, queries, NT) * SCALE2 - rows[j, side : side + 1])
            grads = (weights * (dot(v[part, head], backs, NT) - dots)).astype(BF16)
            dv[part, head] = (dv_far[0, :, head] + dot(weights.astype(BF16), backs, NN)).astype(BF16)
            dk[part, head] = ((dk_far[0, :, head] + dot(grads, queries, NN)) * SCALE).astype(BF16)
            share = dot(grads, keys, TN)
            query_total = share if query_total is None else query_total + share
        dq[0, :, head] = query_total * SCALE


def own_grads(where, q, k, v, back_a, back_b, rows, dots_a, dots_b, far_shares, held, dy0, count):
    full = pl.BlockSpec((SLAB, BLOCK), lambda d, w: (0, lax.rem(w[0] + dy0 + d, 4)))
    sent = pl.BlockSpec((1, TILE + EXTRA, BLOCK), lambda d, w: (dy0 + d, 0, 0))
    half = pl.BlockSpec((1, TILE, BLOCK), lambda d, w: (dy0 + d, 0, 0))
    row = pl.BlockSpec((GROUP, 1, TILE), lambda d, w: (dy0 + d, 0, 0))
    return pl.pallas_call(
        own_kernel,
        grid_spec=pltpu.PrefetchScalarGridSpec(
            num_scalar_prefetch=1,
            grid=(count,),
            in_specs=[
                full,
                full,
                full,
                sent,
                sent,
                pl.BlockSpec((GROUP, 2, SLAB), lambda d, w: (dy0 + d, 0, 0)),
                row,
                row,
            ]
            + [half] * 4
            + [pl.BlockSpec(memory_space=pl.ANY)] * len(held),
            out_specs=[pl.BlockSpec((1, SLAB, BLOCK), lambda d, w: (d, 0, 0)), full, full],
        ),
        out_shape=[jax.ShapeDtypeStruct((count, SLAB, BLOCK), F32)]
        + [jax.ShapeDtypeStruct((SLAB, FEAT), BF16)] * 2,
        input_output_aliases={13: 1, 14: 2} if held else {},
        compiler_params=params(),
        cost_estimate=STEP,
        name="own_grads",
    )(where, q, k, v, back_a, back_b, rows, dots_a, dots_b, *far_shares, *held)


def far_kernel(side, where, q, b, k, v, dq, dk, dv):
    exists = where[3 + side] == 1
    for j in range(GROUP):
        head = columns(j)
        keys = k[:, head]
        queries = q[0, :, head]
        backs = b[0, :TILE, head]
        rows = b[0, TILE:].astype(F32)
        row = sum(rows[j * 5 + i : j * 5 + i + 1] for i in range(3))
        row = jnp.where(exists, row, NEVER)
        dots = rows[j * 5 + 3 : j * 5 + 4] + rows[j * 5 + 4 : j * 5 + 5]
        weights = jnp.exp2(dot(keys, queries, NT) * SCALE2 - row)
        grads = (weights * (dot(v[:, head], backs, NT) - dots)).astype(BF16)
        dq[0, :, head] = (dot(grads, keys, TN) * SCALE).astype(BF16)
        dk[0, :, head] = dot(grads, queries, NN)
        dv[0, :, head] = dot(weights.astype(BF16), backs, NN)


def far_grads(where, side, q, b, k, v):
    edge = pl.BlockSpec((TILE, BLOCK), lambda d, w: (key_tile(side, w), lax.rem(w[0] + d, 4)))
    half = pl.BlockSpec((1, TILE, BLOCK), lambda d, w: (d, 0, 0))
    return pl.pallas_call(
        functools.partial(far_kernel, side),
        grid_spec=pltpu.PrefetchScalarGridSpec(
            num_scalar_prefetch=1,
            grid=(4,),
            in_specs=[
                half,
                pl.BlockSpec((1, TILE + EXTRA, BLOCK), lambda d, w: (d, 0, 0)),
                edge,
                edge,
            ],
            out_specs=[half, half, half],
        ),
        out_shape=[jax.ShapeDtypeStruct((4, TILE, BLOCK), t) for t in (BF16, F32, F32)],
        compiler_params=params(),
        cost_estimate=HIDES,
        name="far_grads",
    )(where, q, b, k, v)


def join_kernel(where, own, first, second, *rest):
    out = rest[-1]
    for side, (start, far) in enumerate(((first_tile, first), (second_tile, second))):
        part = slice(side * TILE, (side + 1) * TILE)
        out[pl.ds(start(where), TILE)] = (own[0, part] + far[0].astype(F32)).astype(BF16)


def join(where, own, first, second, held, dy0, count):
    half = pl.BlockSpec((1, TILE, BLOCK), lambda d, w: (dy0 + d, 0, 0))
    return pl.pallas_call(
        join_kernel,
        grid_spec=pltpu.PrefetchScalarGridSpec(
            num_scalar_prefetch=1,
            grid=(count,),
            in_specs=[pl.BlockSpec((1, SLAB, BLOCK), lambda d, w: (d, 0, 0)), half, half]
            + [pl.BlockSpec(memory_space=pl.ANY)] * len(held),
            out_specs=pl.BlockSpec((SLAB, BLOCK), lambda d, w: (0, lax.rem(w[0] + dy0 + d, 4))),
        ),
        out_shape=jax.ShapeDtypeStruct((SLAB, FEAT), BF16),
        input_output_aliases={4: 0} if held else {},
        compiler_params=params(),
        cost_estimate=STEP,
        name="join_query_grad",
    )(where, own, first, second, *held)


def weight_term_kernel(where, o, g, mine, other):
    product = dot(o[...].T, g[...], NN).astype(BF16)
    y = pl.program_id(0)
    for core in range(2):

        @pl.when(where[2] == core)
        def _():
            for out, holder in ((mine, core), (other, 1 - core)):
                for low in range(2):
                    start = (low * 2 + holder) * ROWS
                    for z in range(4):
                        piece = product[start : start + ROWS, z * QUARTER : (z + 1) * QUARTER]
                        if holder == 0:
                            out[y, z, low] = piece
                        else:
                            out[z, y, low] = piece


def weight_term(where, o, g):
    shape = (4, 4, 2, ROWS, QUARTER)
    whole = pl.BlockSpec(shape, lambda y, w: (0, 0, 0, 0, 0))
    return pl.pallas_call(
        weight_term_kernel,
        grid_spec=pltpu.PrefetchScalarGridSpec(
            num_scalar_prefetch=1,
            grid=(4,),
            in_specs=[
                pl.BlockSpec((SLAB, BLOCK), lambda y, w: (0, y)),
                pl.BlockSpec((SLAB, WIDTH), lambda y, w: (0, 0)),
            ],
            out_specs=[whole, whole],
        ),
        out_shape=[jax.ShapeDtypeStruct(shape, BF16)] * 2,
        compiler_params=params(),
        cost_estimate=HIDES,
        name="weight_term",
    )(where, o, g)


def after(value, *earlier):
    return lax.optimization_barrier((value, *earlier))[0]


def pick(flag, when_zero, when_one):
    return jnp.where(flag == 0, when_zero, when_one)


def split(value, index, axis):
    kept = lax.dynamic_index_in_dim(value, index, axis, keepdims=False)
    given = lax.dynamic_index_in_dim(value, 1 - index, axis, keepdims=False)
    return kept, given


def added(*values):
    return sum(v.astype(F32) for v in values).astype(BF16)


RUNS = ((0, 2), (2, 2))


def body(
    query_rows,
    key_rows,
    value_rows,
    attention_out,
    output_grad,
    output_weight,
    tile_mask,
    live_tiles,
):
    q, k, v, o, g = (
        a[0] for a in (query_rows, key_rows, value_rows, attention_out, output_grad)
    )
    slab = lax.axis_index("seq")
    row = lax.axis_index("dp")
    z = slab // 2
    y = row // 4
    low = (row // 2) % 2
    core = row % 2
    first_slab, last_slab = slab == 0, slab == 7
    lacks_a, lacks_b = pick(core, first_slab, last_slab), pick(core, last_slab, first_slab)
    where = jnp.stack([y, z, core, 1 - lacks_a, 1 - lacks_b]).astype(jnp.int32)

    def query_piece(second, dy0, count):
        start = core * TILE if second else (1 - core) * TILE
        return jnp.stack(
            [
                lax.dynamic_slice(q, (start, ((y + dy0 + d) % 4) * BLOCK), (TILE, BLOCK))
                for d in range(count)
            ]
        )

    quarter = lax.dynamic_slice(output_weight, (0, z * QUARTER), (ROWS, QUARTER))
    partner = send(quarter, SWAP_LOW)
    q = after(q, partner)
    qa = [send(query_piece(False, 0, 2), ROUTE_A)]
    pair = jnp.stack([pick(low, quarter, partner), pick(low, partner, quarter)])
    line = jnp.stack([pair] + [send(pair, from_first(step)) for step in (1, 2, 3)])
    line = after(line, qa[0])
    qa.append(send(query_piece(False, 2, 2), ROUTE_A))
    qb = send(query_piece(True, 0, 4), ROUTE_B)
    plane = jnp.stack([line] + [send(line, from_second(step)) for step in (1, 2, 3)])

    counts = live_tiles[0]
    slabs = jnp.arange(8, dtype=jnp.int32)

    def live(which, tile):
        return jnp.any((slabs == which) & (counts > tile))

    lives = [live(slab - 1, 1), live(slab, 0), live(slab, 1), live(slab + 1, 0)]
    marks = tile_mask[0] == 1
    allowed = [
        [marks[a, b] & lives[a + 1] & lives[a + b] for b in range(3)] for a in range(2)
    ]

    def by_query(lower, upper):
        first, second = pick(core, upper, lower), pick(core, lower, upper)
        return jnp.concatenate(
            [jnp.broadcast_to(first, (1, TILE)), jnp.broadcast_to(second, (1, TILE))], axis=1
        )

    own_allowed = [by_query(allowed[0][1], allowed[1][0]), by_query(allowed[0][2], allowed[1][1])]
    far_allowed = by_query(allowed[0][0], allowed[1][2])
    bias = jnp.where(jnp.concatenate(own_allowed, axis=0), 0.0, -NEVER).astype(F32)

    term_mine, term_other = weight_term(where, after(o, line), g)
    own_row = own_stats(where, after(q, term_mine), k, bias)
    plane = after(plane, qa[1], qb, own_row)
    other = send(plane, SWAP_CORE)
    term_far = send(after(term_other, plane), SWAP_CORE)

    qa = jnp.concatenate(qa, axis=0)
    stat_a = far_stats(where, 0, after(qa, plane), k)
    stat_b = far_stats(where, 1, after(qb, stat_a), k)
    far_row = jnp.concatenate([send(stat_a, ROUTE_B), send(stat_b, ROUTE_A)], axis=2)

    first, second = pick(core, y, z), pick(core, z, y)
    term_far = after(term_far, stat_b)
    rows_shape = (2, ROWS, QUARTER)
    kept, given = split(term_mine.reshape(2, 2, 4, *rows_shape), first % 2, 1)
    kept_far, given_far = split(term_far.reshape(2, 2, 4, *rows_shape), first % 2, 1)
    halves = added(given, given_far)
    g = after(g, halves)
    halves = send(halves, swap_first(1))

    back_a, dots_a = back(where, 0, g, plane, other, o)
    far_row = after(far_row, dots_a)
    far_row = jnp.where(far_allowed[None], far_row, -NEVER)
    top = jnp.maximum(own_row, far_row)
    row_total = top + jnp.log2(jnp.exp2(own_row - top) + jnp.exp2(far_row - top))
    own_rows = jnp.concatenate(
        [
            jnp.where(pick(core, *order)[None], row_total, NEVER)
            for order in (own_allowed, own_allowed[::-1])
        ],
        axis=1,
    )
    far_rows = jnp.where(far_allowed[None], row_total, NEVER)
    back_a = with_statistics(back_a, far_rows[:, :, :TILE], dots_a)
    far_a = send(back_a, ROUTE_A)
    back_b, dots_b = back(where, 1, after(g, back_a), plane, other, o)
    back_b = with_statistics(back_b, far_rows[:, :, TILE:], dots_b)
    far_b = send(back_b, ROUTE_B)

    kept, given = split(added(kept, kept_far, after(halves, back_b)), first // 2, 0)
    qa = after(qa, given)
    halves = send(given, swap_first(2))

    dqa, *share_a = far_grads(where, 0, qa, far_a, k, v)
    returned_a = send(dqa, ROUTE_B)
    kept = added(kept, after(halves, dqa))
    qb = after(qb, kept)

    def block_ahead(step):
        return lax.dynamic_index_in_dim(kept, (second + step) % 4, 0, keepdims=False)

    blocks = [send(block_ahead(step), from_second(4 - step)) for step in (1, 2, 3)]
    dqb, *share_b = far_grads(where, 1, qb, far_b, k, v)
    returned_b = send(dqb, ROUTE_A)

    kept = added(block_ahead(0), *after(tuple(blocks), dqb))
    kept, given = split(kept, low, 0)
    q = after(q, kept)
    beside = send(given, SWAP_LOW)
    returned_a = after(returned_a, kept)
    q = after(q, returned_a)
    arguments = (back_a, back_b, own_rows, dots_a, dots_b, share_a + share_b)
    dq0, *held = own_grads(where, q, k, v, *arguments, (), 0, 2)
    dq1, *held = own_grads(where, after(q, dq0), k, v, *arguments, held, 2, 2)
    both = added(kept, after(beside, dq1))
    both, returned_b = lax.optimization_barrier((both, returned_b))
    both_far = send(both, SWAP_HIGH)
    joined = join(where, dq0, returned_a, returned_b, (), 0, 2)
    whole = (both.astype(F32) + both_far.astype(F32)) * (1.0 / math.sqrt(16 * 6144))

    quarters = jnp.stack([whole] + [send(whole, from_along_z(step)) for step in (1, 2, 3)])
    quarters = jnp.concatenate([quarters, quarters])
    quarters = lax.dynamic_slice_in_dim(quarters, (4 - z) % 4, 4, 0)
    weight_grad = jnp.concatenate([quarters[i] for i in range(4)], axis=1)

    joined = join(where, dq1, returned_a, returned_b, (joined,), 2, 2)
    return joined[None], held[0][None], held[1][None], weight_grad


def solution(mesh):
    in_specs = (
        P("dp", "seq", None),
        P("dp", "seq", None),
        P("dp", "seq", None),
        P("dp", "seq", None),
        P("dp", "seq", None),
        P("dp", None),
        P("dp", "seq", None),
        P("dp", None),
    )
    out_specs = (P("dp", "seq", None), P("dp", "seq", None), P("dp", "seq", None), P("dp", None))
    return jax.shard_map(body, mesh=mesh, in_specs=in_specs, out_specs=out_specs, check_vma=False)
```

```python
import functools
import math

import jax
import jax.numpy as jnp
from jax import lax
from jax.experimental import pallas as pl
from jax.experimental.pallas import tpu as pltpu
from jax.sharding import PartitionSpec as P

HDIM = 128
TILE = 384
SLAB = 768
FEAT = 1536
WIDTH = 3072
GROUP = 3
BLOCK = GROUP * HDIM
QUARTER = WIDTH // 4
ROWS = 96
AXES = ("seq", "dp")
SCALE = 1.0 / math.sqrt(HDIM)
SCALE2 = SCALE / math.log(2.0)
NEVER = 1e30
EXTRA = 16
LIMIT = 48 * 1024 * 1024
F32 = jnp.float32
BF16 = jnp.bfloat16


def place(z, y, x, core):
    return ((z % 4) * 2 + (x % 4) // 2) * 16 + (y % 4) * 4 + (x % 2) * 2 + core


def route(target):
    pairs = []
    for z in range(4):
        for y in range(4):
            for x in range(4):
                for core in range(2):
                    to = target(z, y, x, core)
                    if to is not None:
                        pairs.append((place(z, y, x, core), place(*to)))
    return pairs


def slab_step(step):
    def target(z, y, x, core):
        slab = z * 2 + x // 2 + step
        if slab < 0 or slab > 7:
            return None
        return (slab // 2, y, (slab % 2) * 2 + x % 2, core)

    return route(target)


UP = slab_step(1)
DOWN = slab_step(-1)
CORES = [frozenset(place(z, y, x, core) for z in range(4) for y in range(4) for x in range(4)) for core in range(2)]
ROUTE_A = [p for p in UP if p[0] in CORES[0]] + [p for p in DOWN if p[0] in CORES[1]]
ROUTE_B = [p for p in DOWN if p[0] in CORES[0]] + [p for p in UP if p[0] in CORES[1]]
SWAP_LOW = route(lambda z, y, x, core: (z, y, x ^ 1, core))
SWAP_HIGH = route(lambda z, y, x, core: (z, y, x ^ 2, core))
SWAP_CORE = route(lambda z, y, x, core: (z, y, x, 1 - core))


def from_along_z(step):
    return route(lambda z, y, x, core: (z - step, y, x, core))


def swap_first(bit):
    return route(
        lambda z, y, x, core: (z, y ^ bit, x, core) if core == 0 else (z ^ bit, y, x, core)
    )


def swap_second(bit):
    return route(
        lambda z, y, x, core: (z ^ bit, y, x, core) if core == 0 else (z, y ^ bit, x, core)
    )


def from_first(step):
    return route(
        lambda z, y, x, core: (z, y - step, x, core) if core == 0 else (z - step, y, x, core)
    )


def from_second(step):
    return route(
        lambda z, y, x, core: (z - step, y, x, core) if core == 0 else (z, y - step, x, core)
    )


def send(block, pairs):
    return lax.ppermute(block, AXES, pairs)


def dot(a, b, dims):
    return lax.dot_general(a, b, (dims, ((), ())), preferred_element_type=F32)


NT = ((1,), (1,))
NN = ((1,), (0,))
TN = ((0,), (0,))


def params(**kwargs):
    return pltpu.CompilerParams(vmem_limit_bytes=LIMIT, **kwargs)


HIDES = pl.CostEstimate(flops=100_000_000_000, bytes_accessed=1_000_000, transcendentals=0)
STEP = pl.CostEstimate(flops=100_000_000, bytes_accessed=100_000, transcendentals=0)


def columns(j):
    return slice(j * HDIM, (j + 1) * HDIM)


def first_tile(where):
    return pl.multiple_of((1 - where[2]) * TILE, TILE)


def second_tile(where):
    return pl.multiple_of(where[2] * TILE, TILE)


def own_stats_kernel(where, q, k, bias, out):
    for j in range(GROUP):
        keys = k[:, columns(j)]
        queries = jnp.concatenate(
            [q[pl.ds(start(where), TILE), columns(j)] for start in (first_tile, second_tile)], axis=0
        )
        first = dot(keys[:TILE], queries, NT) * SCALE2 + bias[0:1]
        second = dot(keys[TILE:], queries, NT) * SCALE2 + bias[1:2]
        highest = jnp.maximum(
            jnp.max(first, axis=0, keepdims=True), jnp.max(second, axis=0, keepdims=True)
        )
        total = jnp.sum(jnp.exp2(first - highest), axis=0, keepdims=True) + jnp.sum(
            jnp.exp2(second - highest), axis=0, keepdims=True
        )
        out[j] = highest + jnp.log2(total)


def own_stats(where, q, k, bias):
    wide = pl.BlockSpec((SLAB, BLOCK), lambda d, w: (0, lax.rem(w[0] + d, 4)))
    return pl.pallas_call(
        own_stats_kernel,
        grid_spec=pltpu.PrefetchScalarGridSpec(
            num_scalar_prefetch=1,
            grid=(4,),
            in_specs=[wide, wide, pl.BlockSpec((2, SLAB), lambda d, w: (0, 0))],
            out_specs=pl.BlockSpec((GROUP, 1, SLAB), lambda d, w: (d, 0, 0)),
        ),
        out_shape=jax.ShapeDtypeStruct((12, 1, SLAB), F32),
        compiler_params=params(),
        cost_estimate=STEP,
        name="own_stats",
    )(where, q, k, bias)


def far_stats_kernel(where, q, k, out):
    for j in range(GROUP):
        scores = dot(k[:, columns(j)], q[0, :, columns(j)], NT) * SCALE2
        highest = jnp.max(scores, axis=0, keepdims=True)
        total = jnp.sum(jnp.exp2(scores - highest), axis=0, keepdims=True)
        out[j] = highest + jnp.log2(total)


def key_tile(side, w):
    return w[2] if side == 0 else 1 - w[2]


def far_stats(where, side, q, k):
    return pl.pallas_call(
        far_stats_kernel,
        grid_spec=pltpu.PrefetchScalarGridSpec(
            num_scalar_prefetch=1,
            grid=(4,),
            in_specs=[
                pl.BlockSpec((1, TILE, BLOCK), lambda d, w: (d, 0, 0)),
                pl.BlockSpec((TILE, BLOCK), lambda d, w: (key_tile(side, w), lax.rem(w[0] + d, 4))),
            ],
            out_specs=pl.BlockSpec((GROUP, 1, TILE), lambda d, w: (d, 0, 0)),
        ),
        out_shape=jax.ShapeDtypeStruct((12, 1, TILE), F32),
        compiler_params=params(),
        cost_estimate=STEP,
        name="far_stats",
    )(where, q, k)


def back_kernel(where, g, mine_z, mine_y, other_z, other_y, o, back, dots, weight):
    for core in range(2):

        @pl.when(where[2] == core)
        def _():
            for dz in range(4):
                block = pl.ds(pl.multiple_of(lax.rem(where[1] + dz, 4) * QUARTER, QUARTER), QUARTER)
                for low in range(2):
                    for holder in range(2):
                        if core == holder:
                            piece = mine_z[dz, 0, low] if core == 0 else mine_y[0, dz, low]
                        else:
                            piece = other_y[0, dz, low] if core == 0 else other_z[dz, 0, low]
                        weight[pl.ds((low * 2 + holder) * ROWS, ROWS), block] = piece

    result = dot(g[...], weight[...], NT).astype(BF16)
    back[0, :TILE] = result
    back[0, TILE:] = jnp.zeros((EXTRA, BLOCK), BF16)
    products = result.astype(F32) * o[...].astype(F32)
    coarse = products.astype(BF16)
    fine = (products - coarse.astype(F32)).astype(BF16)
    ones = jnp.ones((8, HDIM), BF16)
    for j in range(GROUP):
        summed = dot(ones, coarse[:, columns(j)], NT) + dot(ones, fine[:, columns(j)], NT)
        dots[j] = summed[0:1]


def back(where, side, g, mine, other, o):
    def tile(w):
        return 1 - w[2] if side == 0 else w[2]

    along_z = pl.BlockSpec((4, 1, 2, ROWS, QUARTER), lambda d, w: (0, d, 0, 0, 0))
    along_y = pl.BlockSpec((1, 4, 2, ROWS, QUARTER), lambda d, w: (d, 0, 0, 0, 0))
    return pl.pallas_call(
        back_kernel,
        grid_spec=pltpu.PrefetchScalarGridSpec(
            num_scalar_prefetch=1,
            grid=(4,),
            in_specs=[
                pl.BlockSpec((TILE, WIDTH), lambda d, w: (tile(w), 0)),
                along_z,
                along_y,
                along_z,
                along_y,
                pl.BlockSpec((TILE, BLOCK), lambda d, w: (tile(w), lax.rem(w[0] + d, 4))),
            ],
            out_specs=[
                pl.BlockSpec((1, TILE + EXTRA, BLOCK), lambda d, w: (d, 0, 0)),
                pl.BlockSpec((GROUP, 1, TILE), lambda d, w: (d, 0, 0)),
            ],
            scratch_shapes=[pltpu.VMEM((BLOCK, WIDTH), BF16)],
        ),
        out_shape=[
            jax.ShapeDtypeStruct((4, TILE + EXTRA, BLOCK), BF16),
            jax.ShapeDtypeStruct((12, 1, TILE), F32),
        ],
        compiler_params=params(),
        cost_estimate=HIDES,
        name="out_back",
    )(where, g, mine, mine, other, other, o)


def pieces(value, count):
    parts = []
    for _ in range(count):
        part = lax.reduce_precision(value, exponent_bits=8, mantissa_bits=7)
        parts.append(part.astype(BF16))
        value = value - part
    return parts


def with_statistics(block, row, dots):
    parts = jnp.concatenate(pieces(row, 3) + pieces(dots, 2), axis=1)
    parts = parts.reshape(4, GROUP * 5, TILE)
    return lax.dynamic_update_slice(block, parts, (0, TILE, 0))


def own_kernel(where, q, k, v, back_a, back_b, rows, dots_a, dots_b, dk_a, dv_a, dk_b, dv_b, *rest):
    dq, dk, dv = rest[-3:]
    for j in range(GROUP):
        head = columns(j)
        queries = jnp.concatenate(
            [q[pl.ds(start(where), TILE), head] for start in (first_tile, second_tile)], axis=0
        )
        backs = jnp.concatenate([back_a[0, :TILE, head], back_b[0, :TILE, head]], axis=0)
        dots = jnp.concatenate([dots_a[j], dots_b[j]], axis=1)
        query_total = None
        sides = ((second_tile, dk_a, dv_a), (first_tile, dk_b, dv_b))
        for side, (start, dk_far, dv_far) in enumerate(sides):
            part = pl.ds(start(where), TILE)
            keys = k[part, head]
            weights = jnp.exp2(dot(keys, queries, NT) * SCALE2 - rows[j, side : side + 1])
            grads = (weights * (dot(v[part, head], backs, NT) - dots)).astype(BF16)
            dv[part, head] = (dv_far[0, :, head] + dot(weights.astype(BF16), backs, NN)).astype(BF16)
            dk[part, head] = ((dk_far[0, :, head] + dot(grads, queries, NN)) * SCALE).astype(BF16)
            share = dot(grads, keys, TN)
            query_total = share if query_total is None else query_total + share
        dq[0, :, head] = query_total * SCALE


def own_grads(where, q, k, v, back_a, back_b, rows, dots_a, dots_b, far_shares, held, dy0, count):
    full = pl.BlockSpec((SLAB, BLOCK), lambda d, w: (0, lax.rem(w[0] + dy0 + d, 4)))
    sent = pl.BlockSpec((1, TILE + EXTRA, BLOCK), lambda d, w: (dy0 + d, 0, 0))
    half = pl.BlockSpec((1, TILE, BLOCK), lambda d, w: (dy0 + d, 0, 0))
    row = pl.BlockSpec((GROUP, 1, TILE), lambda d, w: (dy0 + d, 0, 0))
    return pl.pallas_call(
        own_kernel,
        grid_spec=pltpu.PrefetchScalarGridSpec(
            num_scalar_prefetch=1,
            grid=(count,),
            in_specs=[
                full,
                full,
                full,
                sent,
                sent,
                pl.BlockSpec((GROUP, 2, SLAB), lambda d, w: (dy0 + d, 0, 0)),
                row,
                row,
            ]
            + [half] * 4
            + [pl.BlockSpec(memory_space=pl.ANY)] * len(held),
            out_specs=[pl.BlockSpec((1, SLAB, BLOCK), lambda d, w: (d, 0, 0)), full, full],
        ),
        out_shape=[jax.ShapeDtypeStruct((count, SLAB, BLOCK), F32)]
        + [jax.ShapeDtypeStruct((SLAB, FEAT), BF16)] * 2,
        input_output_aliases={13: 1, 14: 2} if held else {},
        compiler_params=params(),
        cost_estimate=STEP,
        name="own_grads",
    )(where, q, k, v, back_a, back_b, rows, dots_a, dots_b, *far_shares, *held)


def far_kernel(side, where, q, b, k, v, dq, dk, dv):
    exists = where[3 + side] == 1
    for j in range(GROUP):
        head = columns(j)
        keys = k[:, head]
        queries = q[0, :, head]
        backs = b[0, :TILE, head]
        rows = b[0, TILE:].astype(F32)
        row = sum(rows[j * 5 + i : j * 5 + i + 1] for i in range(3))
        row = jnp.where(exists, row, NEVER)
        dots = rows[j * 5 + 3 : j * 5 + 4] + rows[j * 5 + 4 : j * 5 + 5]
        weights = jnp.exp2(dot(keys, queries, NT) * SCALE2 - row)
        grads = (weights * (dot(v[:, head], backs, NT) - dots)).astype(BF16)
        dq[0, :, head] = (dot(grads, keys, TN) * SCALE).astype(BF16)
        dk[0, :, head] = dot(grads, queries, NN)
        dv[0, :, head] = dot(weights.astype(BF16), backs, NN)


def far_grads(where, side, q, b, k, v):
    edge = pl.BlockSpec((TILE, BLOCK), lambda d, w: (key_tile(side, w), lax.rem(w[0] + d, 4)))
    half = pl.BlockSpec((1, TILE, BLOCK), lambda d, w: (d, 0, 0))
    return pl.pallas_call(
        functools.partial(far_kernel, side),
        grid_spec=pltpu.PrefetchScalarGridSpec(
            num_scalar_prefetch=1,
            grid=(4,),
            in_specs=[
                half,
                pl.BlockSpec((1, TILE + EXTRA, BLOCK), lambda d, w: (d, 0, 0)),
                edge,
                edge,
            ],
            out_specs=[half, half, half],
        ),
        out_shape=[jax.ShapeDtypeStruct((4, TILE, BLOCK), t) for t in (BF16, F32, F32)],
        compiler_params=params(),
        cost_estimate=HIDES,
        name="far_grads",
    )(where, q, b, k, v)


def join_kernel(where, own, first, second, *rest):
    out = rest[-1]
    for side, (start, far) in enumerate(((first_tile, first), (second_tile, second))):
        part = slice(side * TILE, (side + 1) * TILE)
        out[pl.ds(start(where), TILE)] = (own[0, part] + far[0].astype(F32)).astype(BF16)


def join(where, own, first, second, held, dy0, count):
    half = pl.BlockSpec((1, TILE, BLOCK), lambda d, w: (dy0 + d, 0, 0))
    return pl.pallas_call(
        join_kernel,
        grid_spec=pltpu.PrefetchScalarGridSpec(
            num_scalar_prefetch=1,
            grid=(count,),
            in_specs=[pl.BlockSpec((1, SLAB, BLOCK), lambda d, w: (d, 0, 0)), half, half]
            + [pl.BlockSpec(memory_space=pl.ANY)] * len(held),
            out_specs=pl.BlockSpec((SLAB, BLOCK), lambda d, w: (0, lax.rem(w[0] + dy0 + d, 4))),
        ),
        out_shape=jax.ShapeDtypeStruct((SLAB, FEAT), BF16),
        input_output_aliases={4: 0} if held else {},
        compiler_params=params(),
        cost_estimate=STEP,
        name="join_query_grad",
    )(where, own, first, second, *held)


def weight_term_kernel(where, o, g, mine, other):
    product = dot(o[...].T, g[...], NN).astype(BF16)
    y = pl.program_id(0)
    for core in range(2):

        @pl.when(where[2] == core)
        def _():
            for out, holder in ((mine, core), (other, 1 - core)):
                for low in range(2):
                    start = (low * 2 + holder) * ROWS
                    for z in range(4):
                        piece = product[start : start + ROWS, z * QUARTER : (z + 1) * QUARTER]
                        if holder == 0:
                            out[y, z, low] = piece
                        else:
                            out[z, y, low] = piece


def weight_term(where, o, g):
    shape = (4, 4, 2, ROWS, QUARTER)
    whole = pl.BlockSpec(shape, lambda y, w: (0, 0, 0, 0, 0))
    return pl.pallas_call(
        weight_term_kernel,
        grid_spec=pltpu.PrefetchScalarGridSpec(
            num_scalar_prefetch=1,
            grid=(4,),
            in_specs=[
                pl.BlockSpec((SLAB, BLOCK), lambda y, w: (0, y)),
                pl.BlockSpec((SLAB, WIDTH), lambda y, w: (0, 0)),
            ],
            out_specs=[whole, whole],
        ),
        out_shape=[jax.ShapeDtypeStruct(shape, BF16)] * 2,
        compiler_params=params(),
        cost_estimate=HIDES,
        name="weight_term",
    )(where, o, g)


def after(value, *earlier):
    return lax.optimization_barrier((value, *earlier))[0]


def pick(flag, when_zero, when_one):
    return jnp.where(flag == 0, when_zero, when_one)


def split(value, index, axis):
    kept = lax.dynamic_index_in_dim(value, index, axis, keepdims=False)
    given = lax.dynamic_index_in_dim(value, 1 - index, axis, keepdims=False)
    return kept, given


def added(*values):
    return sum(v.astype(F32) for v in values).astype(BF16)


RUNS = ((0, 2), (2, 2))


def body(
    query_rows,
    key_rows,
    value_rows,
    attention_out,
    output_grad,
    output_weight,
    tile_mask,
    live_tiles,
):
    q, k, v, o, g = (
        a[0] for a in (query_rows, key_rows, value_rows, attention_out, output_grad)
    )
    slab = lax.axis_index("seq")
    row = lax.axis_index("dp")
    z = slab // 2
    y = row // 4
    low = (row // 2) % 2
    core = row % 2
    first_slab, last_slab = slab == 0, slab == 7
    lacks_a, lacks_b = pick(core, first_slab, last_slab), pick(core, last_slab, first_slab)
    where = jnp.stack([y, z, core, 1 - lacks_a, 1 - lacks_b]).astype(jnp.int32)

    def query_piece(second, dy0, count):
        start = core * TILE if second else (1 - core) * TILE
        return jnp.stack(
            [
                lax.dynamic_slice(q, (start, ((y + dy0 + d) % 4) * BLOCK), (TILE, BLOCK))
                for d in range(count)
            ]
        )

    quarter = lax.dynamic_slice(output_weight, (0, z * QUARTER), (ROWS, QUARTER))
    partner = send(quarter, SWAP_LOW)
    q = after(q, partner)
    qa = [send(query_piece(False, 0, 2), ROUTE_A)]
    pair = jnp.stack([pick(low, quarter, partner), pick(low, partner, quarter)])
    line = jnp.stack([pair] + [send(pair, from_first(step)) for step in (1, 2, 3)])
    line = after(line, qa[0])
    qa.append(send(query_piece(False, 2, 2), ROUTE_A))
    qb = send(query_piece(True, 0, 4), ROUTE_B)
    plane = jnp.stack([line] + [send(line, from_second(step)) for step in (1, 2, 3)])

    counts = live_tiles[0]
    slabs = jnp.arange(8, dtype=jnp.int32)

    def live(which, tile):
        return jnp.any((slabs == which) & (counts > tile))

    lives = [live(slab - 1, 1), live(slab, 0), live(slab, 1), live(slab + 1, 0)]
    marks = tile_mask[0] == 1
    allowed = [
        [marks[a, b] & lives[a + 1] & lives[a + b] for b in range(3)] for a in range(2)
    ]

    def by_query(lower, upper):
        first, second = pick(core, upper, lower), pick(core, lower, upper)
        return jnp.concatenate(
            [jnp.broadcast_to(first, (1, TILE)), jnp.broadcast_to(second, (1, TILE))], axis=1
        )

    own_allowed = [by_query(allowed[0][1], allowed[1][0]), by_query(allowed[0][2], allowed[1][1])]
    far_allowed = by_query(allowed[0][0], allowed[1][2])
    bias = jnp.where(jnp.concatenate(own_allowed, axis=0), 0.0, -NEVER).astype(F32)

    term_mine, term_other = weight_term(where, after(o, line), g)
    own_row = own_stats(where, after(q, term_mine), k, bias)
    plane = after(plane, qa[1], qb, own_row)
    other = send(plane, SWAP_CORE)
    term_far = send(after(term_other, other), SWAP_CORE)

    qa = jnp.concatenate(qa, axis=0)
    stat_a = far_stats(where, 0, after(qa, plane), k)
    stat_b = far_stats(where, 1, after(qb, stat_a), k)
    far_row = jnp.concatenate([send(stat_a, ROUTE_B), send(stat_b, ROUTE_A)], axis=2)

    back_a, dots_a = back(where, 0, g, plane, other, o)
    far_row = after(far_row, dots_a)
    far_row = jnp.where(far_allowed[None], far_row, -NEVER)
    top = jnp.maximum(own_row, far_row)
    row_total = top + jnp.log2(jnp.exp2(own_row - top) + jnp.exp2(far_row - top))
    own_rows = jnp.concatenate(
        [
            jnp.where(pick(core, *order)[None], row_total, NEVER)
            for order in (own_allowed, own_allowed[::-1])
        ],
        axis=1,
    )
    far_rows = jnp.where(far_allowed[None], row_total, NEVER)
    back_a = with_statistics(back_a, far_rows[:, :, :TILE], dots_a)
    far_a = send(back_a, ROUTE_A)
    first, second = pick(core, y, z), pick(core, z, y)
    term_far = after(term_far, back_a)
    rows_shape = (2, ROWS, QUARTER)
    kept, given = split(term_mine.reshape(2, 2, 4, *rows_shape), first % 2, 1)
    kept_far, given_far = split(term_far.reshape(2, 2, 4, *rows_shape), first % 2, 1)
    halves = added(given, given_far)
    g = after(g, halves)
    halves = send(halves, swap_first(1))

    back_b, dots_b = back(where, 1, after(g, back_a), plane, other, o)
    back_b = with_statistics(back_b, far_rows[:, :, TILE:], dots_b)
    far_b = send(back_b, ROUTE_B)

    kept, given = split(added(kept, kept_far, after(halves, back_b)), first // 2, 0)
    qa = after(qa, given)
    halves = send(given, swap_first(2))

    dqa, *share_a = far_grads(where, 0, qa, far_a, k, v)
    returned_a = send(dqa, ROUTE_B)
    kept = added(kept, after(halves, dqa))
    qb = after(qb, kept)

    def block_ahead(step):
        return lax.dynamic_index_in_dim(kept, (second + step) % 4, 0, keepdims=False)

    blocks = [send(block_ahead(step), from_second(4 - step)) for step in (1, 2, 3)]
    dqb, *share_b = far_grads(where, 1, qb, far_b, k, v)
    returned_b = send(dqb, ROUTE_A)

    kept = added(block_ahead(0), *after(tuple(blocks), dqb))
    kept, given = split(kept, low, 0)
    q = after(q, kept)
    beside = send(given, SWAP_LOW)
    returned_a = after(returned_a, kept)
    q = after(q, returned_a)
    arguments = (back_a, back_b, own_rows, dots_a, dots_b, share_a + share_b)
    dq0, *held = own_grads(where, q, k, v, *arguments, (), 0, 2)
    dq1, *held = own_grads(where, after(q, dq0), k, v, *arguments, held, 2, 2)
    both = added(kept, after(beside, dq1))
    both_far = send(both, SWAP_HIGH)
    joined = join(where, dq0, returned_a, returned_b, (), 0, 2)
    whole = (both.astype(F32) + both_far.astype(F32)) * (1.0 / math.sqrt(16 * 6144))

    quarters = jnp.stack([whole] + [send(whole, from_along_z(step)) for step in (1, 2, 3)])
    quarters = jnp.concatenate([quarters, quarters])
    quarters = lax.dynamic_slice_in_dim(quarters, (4 - z) % 4, 4, 0)
    weight_grad = jnp.concatenate([quarters[i] for i in range(4)], axis=1)

    joined = join(where, dq1, returned_a, returned_b, (joined,), 2, 2)
    return joined[None], held[0][None], held[1][None], weight_grad


def solution(mesh):
    in_specs = (
        P("dp", "seq", None),
        P("dp", "seq", None),
        P("dp", "seq", None),
        P("dp", "seq", None),
        P("dp", "seq", None),
        P("dp", None),
        P("dp", "seq", None),
        P("dp", None),
    )
    out_specs = (P("dp", "seq", None), P("dp", "seq", None), P("dp", "seq", None), P("dp", None))
    return jax.shard_map(body, mesh=mesh, in_specs=in_specs, out_specs=out_specs, check_vma=False)
```
